32 devices in a mesh: dp: 2 (over y), ctx: 8 (over z, x), tensor: 2 (over core).
Axes of the slice: x: 2, y: 2, z: 4, core: 2. Of those that a mesh axis runs over, the one named last changes fastest.
Arguments:
- queries: bfloat16 [2048, 8192], P(('dp', 'ctx'), 'tensor'), parts along dimension 0, may hold values from -6 to 6
- keys: bfloat16 [2048, 1024], P(('dp', 'ctx'), 'tensor'), parts along dimension 0, may hold values from -6 to 6
- values: bfloat16 [2048, 1024], P(('dp', 'ctx'), 'tensor'), parts along dimension 0, may hold values from -6 to 6
- attn_out: bfloat16 [2048, 8192], P(('dp', 'ctx'), 'tensor'), parts along dimension 0, may hold values from -6 to 6
- grad_out: bfloat16 [2048, 8192], P(('dp', 'ctx'), 'tensor'), parts along dimension 0, may hold values from -6 to 6
- log_norm: float32 [64, 2048], P('tensor', ('dp', 'ctx')), parts along dimension 1, may hold values from 3 to 6
- doc_lengths: int32 [32], P('dp'), parts along dimension 0, may hold values from 1 to 256, 1024 in all
- block_order: int32 [32], P('dp'), parts along dimension 0, may hold values from 0 to 15, each once
Outputs:
- grad_queries: bfloat16 [2048, 8192], P(('dp', 'ctx'), 'tensor'), parts along dimension 0
- key_gradient_rows: bfloat16 [2048, 1024], P(('dp', 'ctx'), 'tensor'), parts along dimension 0
- value_gradient_rows: bfloat16 [2048, 1024], P(('dp', 'ctx'), 'tensor'), parts along dimension 0
The draws below stay inside these ranges and needn't reach their ends.
There are 2 independent parts, one for each index of `dp`. The reference program is written for one: setup_inputs(seed, part) draws one part's arguments, and reference() takes and returns one part's arrays. A program takes and returns all parts, laid end to end along the dimension named above; each array names one. Nothing has to cross between parts.
Inputs may be any that keep to these rules, and one draw needn't show every extreme that they name: `doc_lengths`: document lengths in sequence order; they sum to 1024 and the largest is exactly 256. `block_order`: each of the 16 blocks of 64 positions appears once.
All inputs are finite; a program needn't handle non-finite values.
Results may differ from the reference program's by a relative error of at most 0.0049.
Values may be sent and summed in bfloat16 or wider, within the bound.
A program may use at most 64 MiB of HBM per device.

```python
import math
import jax
import jax.numpy as jnp
import numpy as np
from jax import lax

QUERY_HEADS = 64
KEY_VALUE_HEADS = 8
HEAD_SIZE = 128
DOCS = 16
PACKED_POSITIONS = 1024
BLOCK = 64
NBLK = 16


def level_of(key, shape, shards, low, high):
    def one(axis_at, parts):
        draws = jax.random.uniform(jax.random.fold_in(jax.random.fold_in(key, 6), axis_at), (parts,), jnp.float32, low / len(shards), high / len(shards))
        return jnp.repeat(jnp.exp(draws), shape[axis_at] // parts).reshape((-1,) + (1,) * (len(shape) - axis_at - 1))

    loudness = one(*shards[0])
    for cut in shards[1:]:
        loudness = loudness * one(*cut)
    return loudness


def length_profile(number_of, total, most, slope):
    loads = [(1 << 20) // math.isqrt(standing ** slope) + 1 for standing in range(2, number_of + 1)]
    rest, holding = total - most - (number_of - 1), [1] * (number_of - 1)
    while rest > 0:
        candidates = [i for i in range(number_of - 1) if holding[i] < most]
        pool, remaining = sum([loads[i] for i in candidates]), rest
        for i in candidates:
            extra = min(most - holding[i], max(1, remaining * loads[i] // pool), rest)
            holding[i] = holding[i] + extra
            rest = rest - extra
    return np.array([most] + holding)


def uneven_parts(rng, amount, total, bound, slope):
    if amount == 2:
        one = jax.random.randint(rng, (), max(1, total - bound), min(bound, total - 1) + 1)
        return jnp.stack([one, total - one])
    sizes = jnp.asarray(length_profile(amount, total, bound, slope), jnp.int32)
    twos = (amount - 1) // 2
    source_of, sink = sizes[1:1 + 2 * twos:2], sizes[2:2 + 2 * twos:2]
    margin = jnp.minimum(source_of - 1, bound - sink)
    passed = jax.random.randint(jax.random.fold_in(rng, 1), (twos,), 0, 1 << 20) % (margin + 1)
    sizes = sizes.at[1:1 + 2 * twos:2].set(source_of - passed).at[2:2 + 2 * twos:2].set(sink + passed)
    return sizes[jax.random.permutation(jax.random.fold_in(rng, 2), amount)]


def centred(rng, shape, scale, most, cuts=(), kind=jnp.bfloat16):
    loudness = level_of(rng, shape, cuts, -0.22, 0.18) if cuts else 1.0
    array = jax.random.normal(rng, shape, jnp.float32) * scale * loudness
    return jnp.minimum(jnp.maximum(array, -most), most).astype(kind)


def setup_inputs(seed: int = 0, part: int = 0) -> dict:
    key_list = jax.random.split(jax.random.key(seed), 9)
    own_keys = jax.random.split(jax.random.fold_in(key_list[8], part), 9)
    queries = centred(own_keys[0], (PACKED_POSITIONS, QUERY_HEADS * HEAD_SIZE), 1.0, 6.0, ((0, 8), (1, 2)))
    keys = centred(own_keys[1], (PACKED_POSITIONS, KEY_VALUE_HEADS * HEAD_SIZE), 1.0, 6.0, ((0, 8), (1, 2)))
    values = centred(own_keys[2], (PACKED_POSITIONS, KEY_VALUE_HEADS * HEAD_SIZE), 1.0, 6.0, ((0, 8), (1, 2)))
    attn_out = centred(own_keys[3], (PACKED_POSITIONS, QUERY_HEADS * HEAD_SIZE), 1.0, 6.0, ((0, 8), (1, 2)))
    grad_out = centred(own_keys[4], (PACKED_POSITIONS, QUERY_HEADS * HEAD_SIZE), 1.0, 6.0, ((0, 8), (1, 2)))
    log_norm = jnp.clip(3.0 + 3.0 * jax.random.uniform(own_keys[5], (QUERY_HEADS, PACKED_POSITIONS), jnp.float32) ** level_of(own_keys[5], (QUERY_HEADS, PACKED_POSITIONS), ((0, 2), (1, 8)), -0.2, 0.2), 3.0, 6.0)
    doc_lengths = uneven_parts(own_keys[6], DOCS, PACKED_POSITIONS, 4 * PACKED_POSITIONS // DOCS, 2).astype(jnp.int32)
    block_order = jax.random.permutation(own_keys[7], NBLK).astype(jnp.int32)
    return dict(queries=queries, keys=keys, values=values, attn_out=attn_out, grad_out=grad_out, log_norm=log_norm, doc_lengths=doc_lengths, block_order=block_order)


def doc_layout(doc_lengths, block_order):
    seq_index = jnp.arange(PACKED_POSITIONS, dtype=jnp.int32)
    position = block_order[seq_index // BLOCK].astype(jnp.int32) * BLOCK + seq_index % BLOCK
    doc_ends = jnp.cumsum(doc_lengths).astype(jnp.int32)
    doc_ids = lax.optimization_barrier(jnp.sum((position[:, None] >= doc_ends[None, :]).astype(jnp.int32), axis=1))
    return (position, doc_ids)

def reference(queries, keys, values, attn_out, grad_out, log_norm, doc_lengths, block_order):
    position, doc_ids = doc_layout(doc_lengths, block_order)
    allowed = (doc_ids[:, None] == doc_ids[None, :]) & (position[None, :] <= position[:, None])
    query_group_width = QUERY_HEADS // KEY_VALUE_HEADS
    score_scale = 1.0 / math.sqrt(HEAD_SIZE)

    def one_head(head_index):
        group_index = head_index // query_group_width
        query_head = lax.dynamic_slice_in_dim(queries, head_index * HEAD_SIZE, HEAD_SIZE, 1)
        out_head = lax.dynamic_slice_in_dim(attn_out, head_index * HEAD_SIZE, HEAD_SIZE, 1)
        grad_head = lax.dynamic_slice_in_dim(grad_out, head_index * HEAD_SIZE, HEAD_SIZE, 1)
        key_head = lax.dynamic_slice_in_dim(keys, group_index * HEAD_SIZE, HEAD_SIZE, 1)
        value_head = lax.dynamic_slice_in_dim(values, group_index * HEAD_SIZE, HEAD_SIZE, 1)
        norm_row = lax.dynamic_index_in_dim(log_norm, head_index, 0, keepdims=False)
        scores = jnp.dot(query_head, key_head.T, preferred_element_type=jnp.float32) * score_scale
        weights = jnp.where(allowed, jnp.exp(scores - norm_row[:, None]), jnp.zeros_like(scores))
        grad_weights = jnp.dot(grad_head, value_head.T, preferred_element_type=jnp.float32)
        out_dot = lax.optimization_barrier(jnp.sum(grad_head.astype(jnp.float32) * out_head.astype(jnp.float32), axis=1))
        grad_scores = (weights * (grad_weights - out_dot[:, None]) * score_scale).astype(jnp.bfloat16)
        weights_bf = weights.astype(jnp.bfloat16)
        grad_query = jnp.dot(grad_scores, key_head, preferred_element_type=jnp.float32).astype(jnp.bfloat16)
        grad_key = jnp.dot(grad_scores.T, query_head, preferred_element_type=jnp.float32)
        grad_value = jnp.dot(weights_bf.T, grad_head, preferred_element_type=jnp.float32)
        return (grad_query, grad_key, grad_value)
    all_query, every_key_row, every_value_row = lax.map(one_head, jnp.arange(QUERY_HEADS, dtype=jnp.int32))
    grad_queries = jnp.transpose(all_query, (1, 0, 2)).reshape(PACKED_POSITIONS, QUERY_HEADS * HEAD_SIZE)
    key_gradient_sum = every_key_row.reshape(KEY_VALUE_HEADS, query_group_width, PACKED_POSITIONS, HEAD_SIZE).sum(axis=1)
    value_gradient_sum = every_value_row.reshape(KEY_VALUE_HEADS, query_group_width, PACKED_POSITIONS, HEAD_SIZE).sum(axis=1)
    key_gradient_rows = jnp.transpose(key_gradient_sum, (1, 0, 2)).reshape(PACKED_POSITIONS, KEY_VALUE_HEADS * HEAD_SIZE).astype(jnp.bfloat16)
    value_gradient_rows = jnp.transpose(value_gradient_sum, (1, 0, 2)).reshape(PACKED_POSITIONS, KEY_VALUE_HEADS * HEAD_SIZE).astype(jnp.bfloat16)
    return (grad_queries, key_gradient_rows, value_gradient_rows)
```

```python
import functools
import math

import jax
import jax.numpy as jnp
from jax import lax
from jax.experimental import pallas as pl
from jax.experimental.pallas import tpu as pltpu
from jax.sharding import PartitionSpec as P

QUERY_HEADS = 64
KEY_VALUE_HEADS = 8
HEAD_SIZE = 128
GROUP = QUERY_HEADS // KEY_VALUE_HEADS
BLOCK = 64
MESH = pl.DeviceIdType.MESH
VMEM_LIMIT = 48 * 1024 * 1024
F32 = jnp.float32
BF16 = jnp.bfloat16


def neighbours(n, visit):
    me = lax.axis_index("ctx")
    row = me // 2
    visit(None, me + 1 - 2 * (me % 2))
    visit(row > 0, me - 2)
    visit(row < n // 2 - 1, me + 2)


def enter(n):
    barrier = pltpu.get_barrier_semaphore()

    def greet(condition, device):
        def signal():
            pl.semaphore_signal(barrier, inc=1, device_id={"ctx": device}, device_id_type=MESH)

        if condition is None:
            signal()
        else:
            pl.when(condition)(signal)

    neighbours(n, greet)
    row = lax.axis_index("ctx") // 2
    ends = (row > 0).astype(jnp.int32) + (row < n // 2 - 1).astype(jnp.int32)
    pl.semaphore_wait(barrier, 1 + ends)


def gather_kernel(n, k_ref, v_ref, all_ref, line_sem, pair_sem, recv_sem):
    lines = n // 2
    me = lax.axis_index("ctx")
    row, col = me // 2, me % 2
    partner = me + 1 - 2 * col
    sources = (k_ref, v_ref)
    enter(n)

    def remote(src, slot, half, sem, device):
        return pltpu.make_async_remote_copy(
            src_ref=src,
            dst_ref=all_ref.at[slot, half],
            send_sem=sem,
            recv_sem=recv_sem.at[slot, half],
            device_id={"ctx": device},
            device_id_type=MESH,
        )

    for half in range(2):
        @pl.when(row > 0)
        def _():
            remote(sources[half], me, half, line_sem.at[0, me, half], me - 2).start()

        @pl.when(row < lines - 1)
        def _():
            remote(sources[half], me, half, line_sem.at[1, me, half], me + 2).start()

        remote(sources[half], me, half, pair_sem.at[me, half], partner).start()
    for half in range(2):
        all_ref[me, half] = sources[half][...]

    def arrived(slot, half):
        remote(all_ref.at[slot, half], slot, half, pair_sem.at[slot, half], partner).wait_recv()

    for step in range(1, lines):
        for half in range(2):
            @pl.when(row - step >= 0)
            def _():
                slot = me - 2 * step
                arrived(slot, half)

                @pl.when(row < lines - 1)
                def _():
                    remote(
                        all_ref.at[slot, half], slot, half, line_sem.at[1, slot, half], me + 2
                    ).start()

                remote(
                    all_ref.at[slot, half], slot, half, pair_sem.at[slot, half], partner
                ).start()

            @pl.when(row + step < lines)
            def _():
                slot = me + 2 * step
                arrived(slot, half)

                @pl.when(row > 0)
                def _():
                    remote(
                        all_ref.at[slot, half], slot, half, line_sem.at[0, slot, half], me - 2
                    ).start()

                remote(
                    all_ref.at[slot, half], slot, half, pair_sem.at[slot, half], partner
                ).start()

    for line in range(lines):
        for half in range(2):
            arrived(2 * line + 1 - col, half)
    for line in range(lines):
        slot = 2 * line + col
        for half in range(2):
            remote(
                all_ref.at[slot, half], slot, half, pair_sem.at[slot, half], partner
            ).wait_send()

            @pl.when((line >= row) & (row > 0))
            def _():
                remote(
                    all_ref.at[slot, half], slot, half, line_sem.at[0, slot, half], me - 2
                ).wait_send()

            @pl.when((line <= row) & (row < lines - 1))
            def _():
                remote(
                    all_ref.at[slot, half], slot, half, line_sem.at[1, slot, half], me + 2
                ).wait_send()


def gather(n, keys, values):
    rows, width = keys.shape
    return pl.pallas_call(
        functools.partial(gather_kernel, n),
        out_shape=jax.ShapeDtypeStruct((n, 2, rows, width), BF16),
        in_specs=[pl.BlockSpec(memory_space=pltpu.VMEM)] * 2,
        out_specs=pl.BlockSpec(memory_space=pltpu.VMEM),
        scratch_shapes=[
            pltpu.SemaphoreType.DMA((2, n, 2)),
            pltpu.SemaphoreType.DMA((n, 2)),
            pltpu.SemaphoreType.DMA((n, 2)),
        ],
        compiler_params=pltpu.CompilerParams(
            collective_id=0, has_side_effects=True, vmem_limit_bytes=VMEM_LIMIT
        ),
        name="gather_kv",
    )(keys, values)


def reduce_kernel(
    n, part_ref, dk_ref, dv_ref, pair_buf, down_buf, up_buf, stage,
    pair_send, pair_recv, line_send, down_recv, up_recv,
):
    lines = n // 2
    me = lax.axis_index("ctx")
    row, col = me // 2, me % 2
    partner = me + 1 - 2 * col
    outs = (dk_ref, dv_ref)
    enter(n)

    def to_partner(line, half):
        return pltpu.make_async_remote_copy(
            src_ref=part_ref.at[2 * line + 1 - col, half],
            dst_ref=pair_buf.at[line, half],
            send_sem=pair_send.at[line, half],
            recv_sem=pair_recv.at[line, half],
            device_id={"ctx": partner},
            device_id_type=MESH,
        )

    def along(line, half, buf, recv, device):
        return pltpu.make_async_remote_copy(
            src_ref=stage.at[line, half],
            dst_ref=buf.at[line, half],
            send_sem=line_send.at[line, half],
            recv_sem=recv.at[line, half],
            device_id={"ctx": device},
            device_id_type=MESH,
        )

    def farthest_first(visit):
        for step in range(lines - 1, 0, -1):
            for half in range(2):
                @pl.when(row - step >= 0)
                def _():
                    visit(row - step, half, -1)

                @pl.when(row + step < lines)
                def _():
                    visit(row + step, half, 1)

    farthest_first(lambda line, half, way: to_partner(line, half).start())
    for half in range(2):
        to_partner(row, half).start()

    def pair_sum(line, half):
        to_partner(line, half).wait_recv()
        own = part_ref[2 * line + col, half].astype(F32)
        return own + pair_buf[line, half].astype(F32)

    def pass_on(line, half, way):
        total = pair_sum(line, half)
        if way < 0:
            stage[line, half] = total.astype(BF16)

            @pl.when(row < lines - 1)
            def _():
                along(line, half, down_buf, down_recv, me - 2).wait_recv()
                stage[line, half] = (total + down_buf[line, half].astype(F32)).astype(BF16)

            along(line, half, down_buf, down_recv, me - 2).start()
        else:
            stage[line, half] = total.astype(BF16)

            @pl.when(row > 0)
            def _():
                along(line, half, up_buf, up_recv, me + 2).wait_recv()
                stage[line, half] = (total + up_buf[line, half].astype(F32)).astype(BF16)

            along(line, half, up_buf, up_recv, me + 2).start()

    farthest_first(pass_on)

    for half in range(2):
        @pl.when(row == 0)
        def _():
            total = pair_sum(row, half)
            along(row, half, down_buf, down_recv, me + 2).wait_recv()
            outs[half][...] = (total + down_buf[row, half].astype(F32)).astype(BF16)

        @pl.when(row == lines - 1)
        def _():
            total = pair_sum(row, half)
            along(row, half, up_buf, up_recv, me - 2).wait_recv()
            outs[half][...] = (total + up_buf[row, half].astype(F32)).astype(BF16)

        @pl.when((row > 0) & (row < lines - 1))
        def _():
            total = pair_sum(row, half)
            along(row, half, down_buf, down_recv, me + 2).wait_recv()
            along(row, half, up_buf, up_recv, me - 2).wait_recv()
            outs[half][...] = (
                total + down_buf[row, half].astype(F32) + up_buf[row, half].astype(F32)
            ).astype(BF16)

    for line in range(lines):
        for half in range(2):
            to_partner(line, half).wait_send()

            @pl.when(row != line)
            def _():
                along(line, half, down_buf, down_recv, partner).wait_send()


def reduce_to_owner(n, parts):
    rows, width = parts.shape[2:]
    lines = n // 2
    buf = pltpu.VMEM((lines, 2, rows, width), BF16)
    sems = pltpu.SemaphoreType.DMA((lines, 2))
    return pl.pallas_call(
        functools.partial(reduce_kernel, n),
        out_shape=[jax.ShapeDtypeStruct((rows, width), BF16)] * 2,
        in_specs=[pl.BlockSpec(memory_space=pltpu.VMEM)],
        out_specs=[pl.BlockSpec(memory_space=pltpu.VMEM)] * 2,
        scratch_shapes=[buf] * 4 + [sems] * 5,
        compiler_params=pltpu.CompilerParams(
            collective_id=1, has_side_effects=True, vmem_limit_bytes=VMEM_LIMIT
        ),
        name="reduce_kv_grads",
    )(parts)


def terms_kernel(
    window, order_ref, lengths_ref, q_ref, o_ref, do_ref, ln_ref, kv_ref,
    dq_ref, part_ref, inverse, terms,
):
    blocks, docs = order_ref.shape[0], lengths_ref.shape[0]
    me = lax.axis_index("ctx")
    scale = 1.0 / math.sqrt(HEAD_SIZE)
    for b in range(blocks):
        inverse[order_ref[b]] = b
    norms = ln_ref[...].reshape(GROUP, 2 * BLOCK).T
    keys_in = window * BLOCK
    nt = (((1,), (1,)), ((), ()))
    tn = (((0,), (0,)), ((), ()))

    def stacked(ref, first):
        return jnp.concatenate(
            [
                ref[first:first + BLOCK, h * HEAD_SIZE:(h + 1) * HEAD_SIZE]
                for h in range(GROUP)
            ],
            axis=0,
        )

    bases = []
    for i in range(2):
        first = i * BLOCK
        at = order_ref[2 * me + i]
        base = at - (window - 1)
        bases.append(base)
        query_pos = at * BLOCK + lax.broadcasted_iota(jnp.int32, (BLOCK, 1), 0)
        start = jnp.zeros((BLOCK, 1), jnp.int32)
        end = jnp.int32(0)
        for d in range(docs):
            end = end + lengths_ref[d]
            start = jnp.where(query_pos >= end, end, start)
        key_pos = base * BLOCK + lax.broadcasted_iota(jnp.int32, (BLOCK, keys_in), 1)
        allowed = ((key_pos >= start) & (key_pos <= query_pos)).astype(F32)
        allowed = jnp.concatenate([allowed] * GROUP, axis=0) > 0.0

        where = [inverse[jnp.maximum(base + w, 0)] for w in range(window)]
        k = jnp.concatenate([kv_ref[b // 2, 0, b % 2] for b in where], axis=0)
        v = jnp.concatenate([kv_ref[b // 2, 1, b % 2] for b in where], axis=0)
        q, o, do = stacked(q_ref, first), stacked(o_ref, first), stacked(do_ref, first)
        dots = jnp.sum(do.astype(F32) * o.astype(F32), axis=1, keepdims=True)
        norm = jnp.concatenate(
            [norms[first:first + BLOCK, h:h + 1] for h in range(GROUP)], axis=0
        )
        scores = lax.dot_general(q, k, nt, preferred_element_type=F32) * scale
        weights = jnp.where(allowed, jnp.exp(scores - norm), 0.0)
        grad_weights = lax.dot_general(do, v, nt, preferred_element_type=F32)
        grad_scores = (weights * (grad_weights - dots) * scale).astype(BF16)
        weights = weights.astype(BF16)
        dq = jnp.dot(grad_scores, k, preferred_element_type=F32).astype(BF16)
        for h in range(GROUP):
            dq_ref[first:first + BLOCK, h * HEAD_SIZE:(h + 1) * HEAD_SIZE] = dq[
                h * BLOCK:(h + 1) * BLOCK
            ]
        dk = lax.dot_general(grad_scores, q, tn, preferred_element_type=F32)
        dv = lax.dot_general(weights, do, tn, preferred_element_type=F32)
        terms[0, i, :window] = dk.reshape(window, BLOCK, HEAD_SIZE)
        terms[1, i, :window] = dv.reshape(window, BLOCK, HEAD_SIZE)
        for kind in range(2):
            terms[kind, i, window] = jnp.zeros((BLOCK, HEAD_SIZE), F32)

    for b in range(blocks):
        slots = []
        for base in bases:
            w = order_ref[b] - base
            slots.append(jnp.where((w >= 0) & (w < window), w, window))
        for kind in range(2):
            part_ref[b // 2, kind, b % 2] = (
                terms[kind, 0, slots[0]] + terms[kind, 1, slots[1]]
            ).astype(BF16)


def terms_of(n, queries, attn_out, grad_out, log_norm, all_kv, doc_lengths, block_order):
    rows, row_width = queries.shape
    local_kv = row_width // (GROUP * HEAD_SIZE)
    blocks = block_order.shape[0]
    window = blocks // 4 + 1
    heads = pl.BlockSpec((rows, GROUP * HEAD_SIZE), lambda g: (0, g))
    pair = pl.BlockSpec((n, 2, 2, BLOCK, HEAD_SIZE), lambda g: (0, 0, 0, 0, g))
    smem = pl.BlockSpec(memory_space=pltpu.SMEM)
    return pl.pallas_call(
        functools.partial(terms_kernel, window),
        grid=(local_kv,),
        out_shape=[
            jax.ShapeDtypeStruct((rows, row_width), BF16),
            jax.ShapeDtypeStruct(all_kv.shape, BF16),
        ],
        in_specs=[
            smem, smem, heads, heads, heads,
            pl.BlockSpec((GROUP, rows), lambda g: (g, 0)),
            pair,
        ],
        out_specs=[heads, pair],
        scratch_shapes=[
            pltpu.SMEM((blocks,), jnp.int32),
            pltpu.VMEM((2, 2, window + 1, BLOCK, HEAD_SIZE), F32),
        ],
        compiler_params=pltpu.CompilerParams(vmem_limit_bytes=VMEM_LIMIT),
        name="attention_terms",
    )(block_order, doc_lengths, queries, attn_out, grad_out, log_norm, all_kv)


def on_device(queries, keys, values, attn_out, grad_out, log_norm, doc_lengths, block_order):
    n = lax.axis_size("ctx")
    rows, width = keys.shape
    all_kv = gather(n, keys, values).reshape(n, 2, 2, BLOCK, width)
    grad_q, parts = terms_of(
        n, queries, attn_out, grad_out, log_norm, all_kv, doc_lengths, block_order
    )
    grad_k, grad_v = reduce_to_owner(n, parts.reshape(n, 2, rows, width))
    return (grad_q, grad_k, grad_v)


def solution(mesh):
    whole = P(("dp", "ctx"), "tensor")
    return jax.shard_map(
        on_device,
        mesh=mesh,
        in_specs=(whole,) * 5 + (P("tensor", ("dp", "ctx")), P("dp"), P("dp")),
        out_specs=(whole,) * 3,
        check_vma=False,
    )
```
